1024 devices in a mesh: fsdp: 32 (over x, y_lo, core), head: 32 (over y_hi, z).
Axes of the slice: x: 8, y: 8 (y_hi: 4, y_lo: 2; y = y_hi * 2 + y_lo), z: 8, core: 2. Of those that a mesh axis runs over, the one named last changes fastest.
Arguments:
- query_nope: float32 [8192, 16384], P('fsdp', 'head'), may hold values from -6 to 6
- query_rope: float32 [8192, 8192], P('fsdp', 'head'), may hold values from -12 to 12
- latent: float32 [8192, 512], P(('fsdp', 'head')), may hold values from -6 to 6
- rope_key: float32 [8192, 64], P(('fsdp', 'head')), may hold values from -4 to 4
- cotangent: float32 [8192, 16384], P('fsdp', 'head'), may hold values from -6 to 6
- bounds: int32 [32, 2], P('fsdp'), may hold values from 1 to 256, as said below
- key_up: float32 [512, 16384], P('fsdp', 'head'), may hold values from -0.25 to 0.25
- value_up: float32 [512, 16384], P('fsdp', 'head'), may hold values from -0.25 to 0.25
Outputs:
- query_nope_grad: float32 [8192, 16384], P('fsdp', 'head')
- query_rope_grad: float32 [8192, 8192], P('fsdp', 'head')
- latent_grad: float32 [8192, 512], P(('fsdp', 'head'))
- rope_key_grad: float32 [8192, 64], P(('fsdp', 'head'))
- key_up_grad: float32 [512, 16384], P('fsdp', 'head')
- value_up_grad: float32 [512, 16384], P('fsdp', 'head')
The draws below stay inside these ranges and needn't reach their ends.
Inputs may be any that keep to these rules, and one draw needn't show every extreme that they name: bounds[s, 0] is the length of sequence s's image prefix, attended in both directions, and bounds[s, 1] its number of valid tokens; 1 <= bounds[s, 0] < 128 < bounds[s, 1]; some sequence has all 256 tokens valid.
All inputs are finite; a program needn't handle non-finite values.
Results may differ from the reference program's by a relative error of at most 0.0003.
Values sent between devices are 32-bit elements; how exact they have to be, the bound alone decides.
A program may use at most 32 MiB of HBM per device.

```python
import jax
import jax.numpy as jnp
from jax import lax

LAT = 512
NOPE = 128
ROPE = 64
VHEAD = 128
SEQ = 256
HEADS = 128
SEQS = 32
TOKENS = 8192


def draw_rope_key(key, part):
    rough = jax.random.truncated_normal(jax.random.fold_in(key, 17), -4.0, 4.0, (TOKENS, ROPE), jnp.float32)
    return rough


def draw_query_rope(key, part):
    rough = jax.random.truncated_normal(jax.random.fold_in(key, 29), -4.0, 4.0, (TOKENS, HEADS, ROPE), jnp.float32)
    return rough.reshape(TOKENS, HEADS * ROPE)


def draw_bounds(key, part):
    prefix = jax.random.randint(jax.random.fold_in(key, 3), (SEQS,), 1, SEQ // 2)
    valid = jax.random.randint(jax.random.fold_in(key, 5), (SEQS,), SEQ // 2 + 2, SEQ + 1)
    valid = jnp.where(jnp.arange(SEQS) == 0, SEQ, valid)
    return jnp.stack([prefix, valid], axis=1).astype(jnp.int32)


def block_scale(rng, extent, cuts, low, top_value):
    factor_of = 1.0
    for dim, shards_of in cuts:
        heights = jax.random.uniform(jax.random.fold_in(jax.random.fold_in(rng, 6), dim), (shards_of,), jnp.float32, low / len(cuts), top_value / len(cuts))
        factor_of = factor_of * jnp.repeat(jnp.exp(heights), extent[dim] // shards_of).reshape((-1,) + (1,) * (len(extent) - 1 - dim))
    return factor_of


def bell_draw(stream_key, dims, scale, most, pieces=(), kind=jnp.bfloat16):
    result = scale * jax.random.normal(stream_key, dims, jnp.float32)
    if pieces:
        result = result * block_scale(stream_key, dims, pieces, -0.22, 0.18)
    return jnp.clip(result, -most, most).astype(kind)


def setup_inputs(seed: int = 0) -> dict:
    arg_keys = jax.random.split(jax.random.key(seed), 9)
    return {
        "query_nope": bell_draw(arg_keys[0], (TOKENS, HEADS * NOPE), 1.0, 6.0, ((0, 32), (1, 32)), jnp.float32),
        "query_rope": draw_query_rope(jax.random.fold_in(arg_keys[8], 71), 0),
        "latent": bell_draw(arg_keys[2], (TOKENS, LAT), 1.0, 6.0, ((0, 1024),), jnp.float32),
        "rope_key": draw_rope_key(jax.random.fold_in(arg_keys[8], 71), 0),
        "cotangent": bell_draw(arg_keys[4], (TOKENS, HEADS * VHEAD), 1.0, 6.0, ((0, 32), (1, 32)), jnp.float32),
        "bounds": draw_bounds(jax.random.fold_in(arg_keys[8], 71), 0),
        "key_up": bell_draw(arg_keys[6], (LAT, HEADS * NOPE), LAT ** -0.5, 0.25, ((0, 32), (1, 32)), jnp.float32),
        "value_up": bell_draw(arg_keys[7], (LAT, HEADS * VHEAD), LAT ** -0.5, 0.25, ((0, 32), (1, 32)), jnp.float32),
    }


HIGHEST = lax.Precision.HIGHEST


def visible_mask(limits, length):
    position = jnp.arange(length)
    query_pos = position[:, None]
    key_pos = position[None, :]
    return (key_pos < limits[1]) & ((key_pos <= query_pos) | (key_pos < limits[0]))


def attention_grads(query_nope, query_rope, key_rows, value_rows, shared_rows, cotangent, limits):
    length = query_nope.shape[0]
    head_count = query_nope.shape[1] // NOPE
    query_nope = query_nope.reshape(length, head_count, NOPE)
    query_rope = query_rope.reshape(length, head_count, ROPE)
    key_rows = key_rows.reshape(length, head_count, NOPE)
    value_rows = value_rows.reshape(length, head_count, VHEAD)
    cotangent = cotangent.reshape(length, head_count, VHEAD)
    factor = (NOPE + ROPE) ** -0.5
    scores = jnp.einsum("ihd,jhd->hij", query_nope, key_rows, precision=HIGHEST)
    scores = (scores + jnp.einsum("ihr,jr->hij", query_rope, shared_rows, precision=HIGHEST)) * factor
    scores = jnp.where(visible_mask(limits, length)[None], scores, -jnp.inf)
    attend = jax.nn.softmax(scores, axis=-1)
    outputs = jnp.einsum("hij,jhv->ihv", attend, value_rows, precision=HIGHEST)
    row_dot = jnp.sum(cotangent * outputs, axis=-1)
    value_grad = jnp.einsum("hij,ihv->jhv", attend, cotangent, precision=HIGHEST)
    grad_attend = jnp.einsum("ihv,jhv->hij", cotangent, value_rows, precision=HIGHEST)
    grad_scores = attend * (grad_attend - jnp.transpose(row_dot)[:, :, None]) * factor
    nope_grad = jnp.einsum("hij,jhd->ihd", grad_scores, key_rows, precision=HIGHEST)
    rope_grad = jnp.einsum("hij,jr->ihr", grad_scores, shared_rows, precision=HIGHEST)
    key_grad = jnp.einsum("hij,ihd->jhd", grad_scores, query_nope, precision=HIGHEST)
    shared_grad = jnp.einsum("hij,ihr->jr", grad_scores, query_rope, precision=HIGHEST)
    return (nope_grad.reshape(length, head_count * NOPE), rope_grad.reshape(length, head_count * ROPE),
            key_grad.reshape(length, head_count * NOPE), value_grad.reshape(length, head_count * VHEAD), shared_grad)


def reference(query_nope, query_rope, latent, rope_key, cotangent, bounds, key_up, value_up):
    seq_count = bounds.shape[0]

    def one_sequence(carry, items):
        nope_rows, rope_rows, latent_rows, shared_rows, cot_rows, limits = items
        key_rows = jnp.dot(latent_rows, key_up, precision=HIGHEST, preferred_element_type=jnp.float32)
        value_rows = jnp.dot(latent_rows, value_up, precision=HIGHEST, preferred_element_type=jnp.float32)
        nope_grad, rope_grad, key_grad, value_grad, shared_grad = attention_grads(
            nope_rows, rope_rows, key_rows, value_rows, shared_rows, cot_rows, limits)
        latent_grad = jnp.dot(key_grad, key_up.T, precision=HIGHEST, preferred_element_type=jnp.float32)
        latent_grad = latent_grad + jnp.dot(value_grad, value_up.T, precision=HIGHEST, preferred_element_type=jnp.float32)
        key_total = carry[0] + jnp.dot(latent_rows.T, key_grad, precision=HIGHEST, preferred_element_type=jnp.float32)
        value_total = carry[1] + jnp.dot(latent_rows.T, value_grad, precision=HIGHEST, preferred_element_type=jnp.float32)
        return (key_total, value_total), (nope_grad, rope_grad, latent_grad, shared_grad)

    items = (query_nope.reshape(seq_count, SEQ, -1), query_rope.reshape(seq_count, SEQ, -1),
             latent.reshape(seq_count, SEQ, -1), rope_key.reshape(seq_count, SEQ, -1),
             cotangent.reshape(seq_count, SEQ, -1), bounds)
    start_sums = (jnp.zeros(key_up.shape, jnp.float32), jnp.zeros(value_up.shape, jnp.float32))
    totals, stacked = lax.scan(one_sequence, start_sums, items)
    return (stacked[0].reshape(seq_count * SEQ, -1), stacked[1].reshape(seq_count * SEQ, -1),
            stacked[2].reshape(seq_count * SEQ, -1), stacked[3].reshape(seq_count * SEQ, -1),
            totals[0], totals[1])
```

```python
import jax
import jax.numpy as jnp
from jax import lax
from jax.experimental import pallas as pl
from jax.experimental.pallas import tpu as pltpu
from jax.sharding import PartitionSpec as P

NOPE = 128
ROPE = 64
VHEAD = 128
SEQ = 256
LAT = 512
LANES = 640
HEADS_HERE = 4
MESH = pl.DeviceIdType.MESH
F32 = jnp.float32
HIGH = lax.Precision.HIGH
FACTOR = (NOPE + ROPE) ** (-0.5)

NX, NYL, NC, NYH, NZ = 8, 2, 2, 4, 8


def dot_nn(a, b):
    return lax.dot_general(a, b, (((1,), (0,)), ((), ())), precision=HIGH, preferred_element_type=F32)


def dot_nt(a, b):
    return lax.dot_general(a, b, (((1,), (1,)), ((), ())), precision=HIGH, preferred_element_type=F32)


class Sems:
    def __init__(self, send, recv):
        self.send, self.recv, self.used = send, recv, 0

    def next(self):
        at = self.used
        self.used += 1
        return self.send.at[at], self.recv.at[at]


N_SEMS = 120


def kernel(
    qn_hbm, qr_hbm, lat_hbm, rk_hbm, cot_hbm, bounds_ref, ku_hbm, vu_hbm,
    qng_hbm, qrg_hbm, lg_hbm, rkg_hbm, kug_hbm, vug_hbm,
    qn, qr, cot, rk, wb, lb, latt, qng, qrg,
    ugb, sb, pb, yb, qb, xr3, xr4, xr1, xr2,
    lgb, zr3, zr4, zr1, zr2, lacc, yr, lgo, rkgo, kugo, vugo,
    send, recv, local,
):
    f = lax.axis_index("fsdp")
    hd = lax.axis_index("head")
    x, y, c = f // 4, (f // 2) % 2, f % 2
    yh, z = hd // NZ, hd % NZ
    sgn = 1 - 2 * c

    def fx(dx):
        return (((x + dx + 2 * NX) % NX * NYL + y) * NC + c, hd)

    to_y = ((x * NYL + (1 - y)) * NC + c, hd)
    to_sib = ((x * NYL + y) * NC + (1 - c), hd)

    def hz(dz):
        return (f, yh * NZ + (z + dz + 2 * NZ) % NZ)

    def hy(r):
        return (f, (yh + r) % NYH * NZ + z)

    def xi(dx):
        return (x + dx + 2 * NX) % NX

    def zi(dz):
        return (z + dz + 2 * NZ) % NZ

    sems = Sems(send, recv)

    def fetch(src, dst, k):
        cp = pltpu.make_async_copy(src, dst, local.at[k])
        cp.start()
        return cp

    c_ku = fetch(ku_hbm, wb.at[f, :, pl.ds(0, 512)], 0)
    c_vu = fetch(vu_hbm, wb.at[f, :, pl.ds(512, 512)], 1)
    c_la = fetch(lat_hbm, lb.at[0, z, :, pl.ds(0, LAT)], 2)
    c_rk = fetch(rk_hbm, rk, 3)
    c_qn = fetch(qn_hbm, qn, 4)
    c_qr = fetch(qr_hbm, qr, 5)
    c_co = fetch(cot_hbm, cot, 6)

    partners = [fx(1), fx(-1), fx(2), fx(-2), to_y, to_sib, hz(1), hz(-1), hz(2), hz(-2), hy(1), hy(2), hy(3)]
    barrier = pltpu.get_barrier_semaphore()
    for p in partners:
        pl.semaphore_signal(barrier, inc=1, device_id=p, device_id_type=MESH)

    c_ku.wait()
    c_vu.wait()
    c_rk.wait()
    c_la.wait()
    lb[0, z, :, pl.ds(LAT, 128)] = jnp.concatenate([rk[...], jnp.zeros((8, 64), F32)], axis=1)
    pl.semaphore_wait(barrier, len(partners))

    started = []

    def push(src, dst, dev):
        s, r = sems.next()
        cp = pltpu.make_async_remote_copy(
            src_ref=src, dst_ref=dst, send_sem=s, recv_sem=r, device_id=dev, device_id_type=MESH
        )
        cp.start()
        started.append(cp)
        return cp

    def wsl(dx, yy, cc):
        return wb.at[(xi(dx) * NYL + yy) * NC + cc]

    def same(ref, dev):
        return push(ref, ref, dev)

    own_w = wsl(0, y, c)
    own_l = lb.at[0, z]

    def lb_r(r):
        return lb.at[r, z]

    ly = [push(own_l, lb_r(NYH - r), hy(r)) for r in (1, 2, 3)]
    xa = {}
    za = {}
    za[2] = same(own_l, hz(2))
    za[-2] = same(own_l, hz(-2))
    xa[2] = same(own_w, fx(2))
    xa[-2] = same(own_w, fx(-2))
    za[1] = same(own_l, hz(1))
    za[-1] = same(own_l, hz(-1))
    ya = {0: same(own_w, to_y)}
    xa[1] = same(own_w, fx(1))
    xa[-1] = same(own_w, fx(-1))
    sa = {("x", 0): same(own_w, to_sib)}

    for cp in ly:
        cp.wait_recv()
    rest = lb.at[pl.ds(1, 3), z]
    zb = {d: same(rest, hz(d)) for d in (2, -2, 1, -1)}

    for d in (1, -1):
        xa[d].wait_recv()
        ya[-d] = same(wsl(-d, y, c), to_y)
        sa[("x", -d)] = same(wsl(-d, y, c), to_sib)
    ya[0].wait_recv()
    sa[("y", 0)] = same(wsl(0, 1 - y, c), to_sib)
    for d in (2, -2):
        xa[d].wait_recv()
        xa[d + d // 2] = same(wsl(-d, y, c), fx(d // 2))
    xa[4] = same(wsl(-2 * sgn, y, c), fx(2 * sgn))
    for d in (2, -2):
        ya[-d] = same(wsl(-d, y, c), to_y)
        sa[("x", -d)] = same(wsl(-d, y, c), to_sib)
    for d in (2, -2):
        za[d].wait_recv()
        zb[d].wait_recv()
        za[d + d // 2] = same(lb.at[:, zi(-d)], hz(d // 2))
    za[4] = same(lb.at[:, zi(-2 * sgn)], hz(2 * sgn))
    for d in (1, -1):
        ya[d].wait_recv()
        sa[("y", d)] = same(wsl(d, 1 - y, c), to_sib)
    for d in (3, -3):
        xa[d].wait_recv()
        ya[-d] = same(wsl(-d, y, c), to_y)
        sa[("x", -d)] = same(wsl(-d, y, c), to_sib)
    xa[4].wait_recv()
    ya[4] = same(wsl(4, y, c), to_y)
    sa[("x", 4)] = same(wsl(4, y, c), to_sib)
    for d in (2, -2):
        ya[d].wait_recv()
        sa[("y", d)] = same(wsl(d, 1 - y, c), to_sib)
    for d in (1, -1):
        za[d].wait_recv()
        zb[d].wait_recv()
    for d in (3, -3, 4):
        za[d].wait_recv()
    for d in (3, -3, 4):
        ya[d].wait_recv()
        sa[("y", d)] = same(wsl(d, 1 - y, c), to_sib)
    c_qn.wait()
    c_qr.wait()
    c_co.wait()

    lat = lb[:, :, :, pl.ds(0, LAT)].reshape(SEQ, LAT)
    rope = lb[:, :, :, pl.ds(LAT, 128)].reshape(SEQ, 128)[:, :ROPE]
    latt[...] = lat.T
    for cp in sa.values():
        cp.wait_recv()

    row = lax.broadcasted_iota(jnp.int32, (SEQ, SEQ), 0)
    query = lax.broadcasted_iota(jnp.int32, (SEQ, SEQ), 1)
    turned = row + yh * 64
    key = jnp.where(turned >= SEQ, turned - SEQ, turned)
    visible = (key < bounds_ref[0, 1]) & ((key <= query) | (key < bounds_ref[0, 0]))

    def kv_up(h):
        a = wb[:, :, pl.ds(h * NOPE, NOPE)].reshape(LAT, NOPE)
        b = wb[:, :, pl.ds(512 + h * VHEAD, VHEAD)].reshape(LAT, VHEAD)
        return jnp.concatenate([a, b], axis=1)

    s1, s2, s3, s4, s5 = {}, {}, {}, {}, {}

    def stage1(h):
        s1[h] = push(ugb.at[h, :, 1 - c], sb.at[h], to_sib)

    def stage2(h):
        s1[h].wait_recv()
        pb[h] = ugb[h, :, pl.ds(c, 1)].reshape(8, 2, 16, 256) + sb[h].reshape(8, 2, 16, 256)
        s2[h] = push(pb.at[h, :, 1 - y], yb.at[h], to_y)

    def stage3(h):
        s2[h].wait_recv()
        qb[h] = pb[h, :, pl.ds(y, 1)].reshape(8, 16, 256) + yb[h]
        s3[h] = (
            push(qb.at[h, xi(3)], xr3.at[h, 0], fx(1)),
            push(qb.at[h, xi(-3)], xr3.at[h, 1], fx(-1)),
            push(qb.at[h, xi(4)], xr4.at[h], fx(2 * sgn)),
        )
        s4[h] = [
            push(qb.at[h, xi(1)], xr1.at[h, 0], fx(1)),
            push(qb.at[h, xi(-1)], xr1.at[h, 1], fx(-1)),
        ]

    def stage4(h):
        for cp in s3[h]:
            cp.wait_recv()
        xr2_own = [qb[h, xi(2)] + xr3[h, 0], qb[h, xi(-2)] + xr3[h, 1]]
        qb[h, xi(2)] = xr2_own[0]
        qb[h, xi(-2)] = xr2_own[1]
        qb[h, xi(2 * sgn)] = qb[h, xi(2 * sgn)] + xr4[h]
        s4[h] += [
            push(qb.at[h, xi(2)], xr2.at[h, 0], fx(2)),
            push(qb.at[h, xi(-2)], xr2.at[h, 1], fx(-2)),
        ]

    def stage5(h):
        for cp in s4[h]:
            cp.wait_recv()
        total = qb[h, x] + (xr1[h, 0] + xr1[h, 1]) + (xr2[h, 0] + xr2[h, 1])
        kugo[:, pl.ds(h * NOPE, NOPE)] = total[:, :NOPE]
        vugo[:, pl.ds(h * VHEAD, VHEAD)] = total[:, NOPE:]

    shared = None
    latent_term = None
    outs = []
    rope_grads = []
    for h in range(HEADS_HERE):
        up = kv_up(h)
        kv = dot_nn(lat, up)
        kk = jnp.concatenate([kv[:, :NOPE], rope], axis=1)
        vv = kv[:, NOPE:]
        q = jnp.concatenate([qn[:, pl.ds(h * NOPE, NOPE)], qr[:, h * ROPE : (h + 1) * ROPE]], axis=1)
        ct = cot[:, pl.ds(h * VHEAD, VHEAD)]
        scores = dot_nt(kk, q) * FACTOR
        scores = jnp.where(visible, scores, -jnp.inf)
        top = jnp.max(scores, axis=0, keepdims=True)
        attend = jnp.exp(scores - top)
        attend = attend / jnp.sum(attend, axis=0, keepdims=True)
        grad_attend = dot_nt(vv, ct)
        row_dot = jnp.sum(attend * grad_attend, axis=0, keepdims=True)
        grad_scores = attend * (grad_attend - row_dot) * FACTOR
        vg = dot_nn(attend, ct)
        kg = dot_nn(grad_scores, q)
        qg = dot_nn(grad_scores.T, kk)
        qng[:, pl.ds(h * NOPE, NOPE)] = qg[:, :NOPE]
        rope_grads.append(qg[:, NOPE:])
        shared = kg[:, NOPE:] if shared is None else shared + kg[:, NOPE:]
        both = jnp.concatenate([kg[:, :NOPE], vg], axis=1)
        term = dot_nt(both, up)
        latent_term = term if latent_term is None else latent_term + term
        if h == HEADS_HERE - 1:
            lgb[:, :, :, pl.ds(0, LAT)] = latent_term.reshape(NYH, NZ, 8, LAT)
            lgb[:, :, :, pl.ds(LAT, 128)] = jnp.concatenate(
                [shared, jnp.zeros((SEQ, 64), F32)], axis=1
            ).reshape(NYH, NZ, 8, 128)
            l3 = (
                push(lgb.at[:, zi(3)], zr3.at[0], hz(1)),
                push(lgb.at[:, zi(-3)], zr3.at[1], hz(-1)),
                push(lgb.at[:, zi(4)], zr4, hz(2 * sgn)),
            )
            l1 = [
                push(lgb.at[:, zi(1)], zr1.at[0], hz(1)),
                push(lgb.at[:, zi(-1)], zr1.at[1], hz(-1)),
            ]
        ugb[h] = dot_nn(latt[...], both).reshape(16, 2, 16, 256)
        stage1(h)
        if h % 2 == 1:
            qrg[:, pl.ds((h - 1) * ROPE, 128)] = jnp.concatenate(rope_grads[-2:], axis=1)
        if h >= 1:
            stage2(h - 1)
        if h >= 2:
            stage3(h - 2)
        if h >= 3:
            stage4(h - 3)

    def put(src, dst, k):
        cp = pltpu.make_async_copy(src, dst, local.at[k])
        cp.start()
        outs.append(cp)

    put(qng, qng_hbm, 7)
    put(qrg, qrg_hbm, 8)
    stage2(3)
    stage3(2)
    stage4(1)
    stage5(0)
    for cp in l3:
        cp.wait_recv()
    lgb[:, pl.ds(zi(2), 1)] = lgb[:, pl.ds(zi(2), 1)] + zr3[0].reshape(NYH, 1, 8, LANES)
    lgb[:, pl.ds(zi(-2), 1)] = lgb[:, pl.ds(zi(-2), 1)] + zr3[1].reshape(NYH, 1, 8, LANES)
    lgb[:, pl.ds(zi(2 * sgn), 1)] = lgb[:, pl.ds(zi(2 * sgn), 1)] + zr4[...].reshape(NYH, 1, 8, LANES)
    l1 += [
        push(lgb.at[:, zi(2)], zr2.at[0], hz(2)),
        push(lgb.at[:, zi(-2)], zr2.at[1], hz(-2)),
    ]
    stage3(3)
    stage4(2)
    stage5(1)
    for cp in l1:
        cp.wait_recv()
    lacc[...] = (
        lgb[:, pl.ds(z, 1)].reshape(NYH, 8, LANES) + (zr1[0] + zr1[1]) + (zr2[0] + zr2[1])
    )
    l4 = [push(lacc.at[r], yr.at[r - 1], hy(r)) for r in (1, 2, 3)]
    stage4(3)
    stage5(2)
    for cp in l4:
        cp.wait_recv()
    total = (lacc[0] + yr[0]) + (yr[1] + yr[2])
    lgo[...] = total[:, :LAT]
    rkgo[...] = total[:, LAT : LAT + ROPE]
    put(lgo, lg_hbm, 9)
    put(rkgo, rkg_hbm, 10)
    stage5(3)
    put(kugo, kug_hbm, 11)
    put(vugo, vug_hbm, 12)
    for cp in started:
        cp.wait_send()
    for cp in outs:
        cp.wait()


def hand_over(*refs):
    for a, b in zip(refs[:6], refs[6:]):
        b[...] = a[...]


def on_device(query_nope, query_rope, latent, rope_key, cotangent, bounds, key_up, value_up):
    shapes = [
        (SEQ, 512), (SEQ, 256), (8, LAT), (8, ROPE), (16, 512), (16, 512),
    ]
    out_shape = [jax.ShapeDtypeStruct(s, F32) for s in shapes]
    hbm = pl.BlockSpec(memory_space=pl.ANY)
    vm = lambda *s: pltpu.VMEM(s, F32)
    results = pl.pallas_call(
        kernel,
        out_shape=out_shape,
        in_specs=[hbm] * 5 + [pl.BlockSpec(memory_space=pltpu.SMEM)] + [hbm] * 2,
        out_specs=[hbm] * 6,
        scratch_shapes=[
            vm(SEQ, 512), vm(SEQ, 256), vm(SEQ, 512), vm(8, ROPE),
            vm(32, 16, 1024), vm(NYH, NZ, 8, LANES), vm(LAT, SEQ), vm(SEQ, 512), vm(SEQ, 256),
            vm(4, 16, 2, 16, 256), vm(4, 16, 16, 256), vm(4, 8, 2, 16, 256), vm(4, 8, 16, 256),
            vm(4, 8, 16, 256), vm(4, 2, 16, 256), vm(4, 16, 256), vm(4, 2, 16, 256), vm(4, 2, 16, 256),
            vm(NYH, NZ, 8, LANES), vm(2, NYH, 8, LANES), vm(NYH, 8, LANES),
            vm(2, NYH, 8, LANES), vm(2, NYH, 8, LANES), vm(NYH, 8, LANES), vm(3, 8, LANES),
            vm(8, LAT), vm(8, ROPE), vm(16, 512), vm(16, 512),
            pltpu.SemaphoreType.DMA((N_SEMS,)),
            pltpu.SemaphoreType.DMA((N_SEMS,)),
            pltpu.SemaphoreType.DMA((13,)),
        ],
        compiler_params=pltpu.CompilerParams(
            collective_id=0, has_side_effects=True, vmem_limit_bytes=60 * 2**20
        ),
        name="fused",
    )(query_nope, query_rope, latent, rope_key, cotangent, bounds, key_up, value_up)
    whole = pl.BlockSpec(memory_space=pltpu.VMEM)
    return pl.pallas_call(
        hand_over,
        out_shape=out_shape,
        in_specs=[whole] * 6,
        out_specs=[whole] * 6,
        compiler_params=pltpu.CompilerParams(vmem_limit_bytes=60 * 2**20),
        name="hand_over",
    )(*results)


def solution(mesh):
    return jax.shard_map(
        on_device,
        mesh=mesh,
        in_specs=(
            P("fsdp", "head"),
            P("fsdp", "head"),
            P(("fsdp", "head"), None),
            P(("fsdp", "head"), None),
            P("fsdp", "head"),
            P("fsdp", None),
            P("fsdp", "head"),
            P("fsdp", "head"),
        ),
        out_specs=(
            P("fsdp", "head"),
            P("fsdp", "head"),
            P(("fsdp", "head"), None),
            P(("fsdp", "head"), None),
            P("fsdp", "head"),
            P("fsdp", "head"),
        ),
        check_vma=False,
    )
```

```python
import jax
import jax.numpy as jnp
from jax import lax
from jax.experimental import pallas as pl
from jax.experimental.pallas import tpu as pltpu
from jax.sharding import PartitionSpec as P

NOPE = 128
ROPE = 64
VHEAD = 128
SEQ = 256
LAT = 512
LANES = 640
HEADS_HERE = 4
MESH = pl.DeviceIdType.MESH
F32 = jnp.float32
HIGH = lax.Precision.HIGH
FACTOR = (NOPE + ROPE) ** (-0.5)

NX, NYL, NC, NYH, NZ = 8, 2, 2, 4, 8


def dot_nn(a, b):
    return lax.dot_general(a, b, (((1,), (0,)), ((), ())), precision=HIGH, preferred_element_type=F32)


def dot_nt(a, b):
    return lax.dot_general(a, b, (((1,), (1,)), ((), ())), precision=HIGH, preferred_element_type=F32)


N_SEMS = 128


def kernel(
    qn_hbm, qr_hbm, lat_hbm, rk_hbm, cot_hbm, bounds_ref, ku_hbm, vu_hbm,
    qng_hbm, qrg_hbm, lg_hbm, rkg_hbm, kug_hbm, vug_hbm,
    qn, qr, cot, rk, wb, lb, latt, qng, qrg,
    ugb, sb, pb, yb, qb, xr,
    lgb, zr3, zr4, zr1, zr2, lacc, yr, lgo, rkgo, kugo, vugo,
    send, recv, local,
):
    f = lax.axis_index("fsdp")
    hd = lax.axis_index("head")
    x, y, c = f // 4, (f // 2) % 2, f % 2
    yh, z = hd // NZ, hd % NZ
    sgn = 1 - 2 * c

    def xi(dx):
        return (x + dx + 2 * NX) % NX

    def zi(dz):
        return (z + dz + 2 * NZ) % NZ

    def fx(dx):
        return ((xi(dx) * NYL + y) * NC + c, hd)

    def hz(dz):
        return (f, yh * NZ + zi(dz))

    def hy(r):
        return (f, (yh + r) % NYH * NZ + z)

    to_y = ((x * NYL + (1 - y)) * NC + c, hd)
    to_sib = ((x * NYL + y) * NC + (1 - c), hd)
    around = (2, -2, 3, -3, 4, 1, -1)

    n_local = [0]

    def on_device_copy(src, dst):
        cp = pltpu.make_async_copy(src, dst, local.at[n_local[0]])
        n_local[0] += 1
        cp.start()
        return cp

    started = []

    def push(src, dst, dev):
        k = len(started)
        cp = pltpu.make_async_remote_copy(
            src_ref=src, dst_ref=dst, send_sem=send.at[k], recv_sem=recv.at[k], device_id=dev, device_id_type=MESH
        )
        cp.start()
        started.append(cp)
        return cp

    def same(ref, dev):
        return push(ref, ref, dev)

    def landed(copies):
        for cp in copies:
            cp.wait_recv()

    own = [on_device_copy(lat_hbm, lb.at[0, z, :, pl.ds(0, LAT)]), on_device_copy(rk_hbm, rk)]
    for h in range(HEADS_HERE):
        own.append(on_device_copy(ku_hbm.at[:, pl.ds(h * NOPE, NOPE)], wb.at[h, x, y, c, :, pl.ds(0, NOPE)]))
        own.append(on_device_copy(vu_hbm.at[:, pl.ds(h * VHEAD, VHEAD)], wb.at[h, x, y, c, :, pl.ds(NOPE, VHEAD)]))
    later = [on_device_copy(qn_hbm, qn), on_device_copy(qr_hbm, qr), on_device_copy(cot_hbm, cot)]

    partners = [fx(d) for d in around] + [to_y, to_sib] + [hz(d) for d in around] + [hy(r) for r in (1, 2, 3)]
    barrier = pltpu.get_barrier_semaphore()
    for p in partners:
        pl.semaphore_signal(barrier, inc=1, device_id=p, device_id_type=MESH)
    for cp in own:
        cp.wait()
    lb[0, z, :, pl.ds(LAT, 128)] = jnp.concatenate([rk[...], jnp.zeros((8, 64), F32)], axis=1)
    pl.semaphore_wait(barrier, len(partners))

    ly = {r: push(lb.at[0, z], lb.at[NYH - r, z], hy(r)) for r in (1, 3, 2)}
    za = {d: same(lb.at[0, z], hz(d)) for d in around}
    xa, ya, sx, sy = {}, {}, {}, {}
    for h in range(HEADS_HERE):
        xa[h] = [same(wb.at[h, x, y, c], fx(d)) for d in around]
    zb = {d: [] for d in around}
    for r in (1, 3, 2):
        ly[r].wait_recv()
        for d in (2, -2, 1, -1):
            zb[d].append(same(lb.at[NYH - r, z], hz(d)))

    def row_over(h):
        landed(xa[h])
        ya[h] = same(wb.at[h, :, y, c], to_y)
        sx[h] = same(wb.at[h, :, y, c], to_sib)

    def other_row_over(h):
        ya[h].wait_recv()
        sy[h] = same(wb.at[h, :, 1 - y, c], to_sib)

    row_over(0)
    for d in (2, -2):
        landed(zb[d])
        zb[d + d // 2].append(same(lb.at[pl.ds(1, 3), zi(-d)], hz(d // 2)))
    zb[4].append(same(lb.at[pl.ds(1, 3), zi(-2 * sgn)], hz(2 * sgn)))
    row_over(1)
    other_row_over(0)
    row_over(2)
    for d in around:
        za[d].wait_recv()
    landed(zb[1] + zb[-1])
    landed(zb[3] + zb[-3] + zb[4])
    for cp in later:
        cp.wait()

    lat = lb[:, :, :, pl.ds(0, LAT)].reshape(SEQ, LAT)
    rope = lb[:, :, :, pl.ds(LAT, 128)].reshape(SEQ, 128)[:, :ROPE]

    row = lax.broadcasted_iota(jnp.int32, (SEQ, SEQ), 0)
    query = lax.broadcasted_iota(jnp.int32, (SEQ, SEQ), 1)
    turned = row + yh * 64
    key = jnp.where(turned >= SEQ, turned - SEQ, turned)
    visible = (key < bounds_ref[0, 1]) & ((key <= query) | (key < bounds_ref[0, 0]))

    s1, s2, s3 = {}, {}, {}

    def stage1(h):
        ugb[h] = dot_nn(latt[...], both[h]).reshape(16, 2, 16, 256)
        s1[h] = push(ugb.at[h, :, 1 - c], sb.at[h], to_sib)

    def stage2(h):
        s1[h].wait_recv()
        pb[h] = ugb[h, :, pl.ds(c, 1)].reshape(8, 2, 16, 256) + sb[h].reshape(8, 2, 16, 256)
        s2[h] = push(pb.at[h, :, 1 - y], yb.at[h], to_y)

    def stage3(h):
        s2[h].wait_recv()
        qb[h] = pb[h, :, pl.ds(y, 1)].reshape(8, 16, 256) + yb[h]
        s3[h] = [push(qb.at[h, xi(d)], xr.at[h, k], fx(d)) for k, d in enumerate(around)]

    def stage4(h):
        landed(s3[h])
        total = (qb[h, x] + xr[h, 0]) + (xr[h, 1] + xr[h, 2])
        total = total + ((xr[h, 3] + xr[h, 4]) + (xr[h, 5] + xr[h, 6]))
        kugo[:, pl.ds(h * NOPE, NOPE)] = total[:, :NOPE]
        vugo[:, pl.ds(h * VHEAD, VHEAD)] = total[:, NOPE:]

    both = {}
    rope_grads = []
    shared = latent_term = None
    for h in range(HEADS_HERE):
        landed([sx[h], sy[h]])
        up = wb[h].reshape(LAT, 256)
        kv = dot_nn(lat, up)
        if h == 0:
            latt[...] = lat.T
        kk = jnp.concatenate([kv[:, :NOPE], rope], axis=1)
        vv = kv[:, NOPE:]
        q = jnp.concatenate([qn[:, pl.ds(h * NOPE, NOPE)], qr[:, h * ROPE : (h + 1) * ROPE]], axis=1)
        ct = cot[:, pl.ds(h * VHEAD, VHEAD)]
        scores = dot_nt(kk, q) * FACTOR
        scores = jnp.where(visible, scores, -jnp.inf)
        top = jnp.max(scores, axis=0, keepdims=True)
        attend = jnp.exp(scores - top)
        attend = attend * (1.0 / jnp.sum(attend, axis=0, keepdims=True))
        grad_attend = dot_nt(vv, ct)
        row_dot = jnp.sum(attend * grad_attend, axis=0, keepdims=True)
        grad_scores = attend * (grad_attend - row_dot) * FACTOR
        vg = dot_nn(attend, ct)
        kg = dot_nn(grad_scores, q)
        qg = dot_nn(grad_scores.T, kk)
        qng[:, pl.ds(h * NOPE, NOPE)] = qg[:, :NOPE]
        rope_grads.append(qg[:, NOPE:])
        shared = kg[:, NOPE:] if shared is None else shared + kg[:, NOPE:]
        both[h] = jnp.concatenate([kg[:, :NOPE], vg], axis=1)
        if h % 2 == 1:
            qrg[:, pl.ds((h - 1) * ROPE, 128)] = jnp.concatenate(rope_grads[-2:], axis=1)
        if h == 0:
            row_over(3)
        if h < 3:
            other_row_over(h + 1)
        term = dot_nt(both[h], up)
        latent_term = term if latent_term is None else latent_term + term
        if h < 3:
            if h > 0:
                stage2(h - 1)
            stage1(h)

    lgb[pl.ds(0, 3), :, :, pl.ds(0, LAT)] = latent_term[64:].reshape(3, NZ, 8, LAT)
    lgb[3, :, :, pl.ds(0, LAT)] = latent_term[:64].reshape(NZ, 8, LAT)
    shared = jnp.concatenate([shared, jnp.zeros((SEQ, 64), F32)], axis=1)
    lgb[pl.ds(0, 3), :, :, pl.ds(LAT, 128)] = shared[64:].reshape(3, NZ, 8, 128)
    lgb[3, :, :, pl.ds(LAT, 128)] = shared[:64].reshape(NZ, 8, 128)
    l3, l1 = {}, {}
    for g in (0, 1):
        part = pl.ds(2 * g, 2)
        l3[g] = [
            push(lgb.at[part, zi(4)], zr4.at[part], hz(2 * sgn)),
            push(lgb.at[part, zi(3)], zr3.at[0, part], hz(1)),
            push(lgb.at[part, zi(-3)], zr3.at[1, part], hz(-1)),
        ]
        l1[g] = [
            push(lgb.at[part, zi(1)], zr1.at[0, part], hz(1)),
            push(lgb.at[part, zi(-1)], zr1.at[1, part], hz(-1)),
        ]

    def latent_step2(g):
        landed(l3[g])
        part = pl.ds(2 * g, 2)
        for k, d in enumerate((2, -2)):
            at = (part, pl.ds(zi(d), 1))
            lgb[at] = lgb[at] + zr3[k, part].reshape(2, 1, 8, LANES)
        at = (part, pl.ds(zi(2 * sgn), 1))
        lgb[at] = lgb[at] + zr4[part].reshape(2, 1, 8, LANES)
        l1[g] += [push(lgb.at[part, zi(d)], zr2.at[k, part], hz(d)) for k, d in enumerate((2, -2))]

    l4 = []

    def latent_step3(g):
        landed(l1[g])
        part = pl.ds(2 * g, 2)
        lacc[part] = (
            lgb[part, pl.ds(z, 1)].reshape(2, 8, LANES) + (zr1[0, part] + zr1[1, part]) + (zr2[0, part] + zr2[1, part])
        )
        for p in (2 * g + 1, 2 * g):
            if p < 3:
                l4.append(push(lacc.at[p], yr.at[p], hy(p + 1)))

    outs = []
    stage1(3)
    stage2(2)
    stage3(0)
    stage2(3)
    outs.append(on_device_copy(qng, qng_hbm))
    outs.append(on_device_copy(qrg, qrg_hbm))
    stage3(1)
    latent_step2(0)
    stage3(2)
    latent_step2(1)
    stage3(3)
    latent_step3(0)
    latent_step3(1)
    stage4(0)
    stage4(1)
    stage4(2)
    landed(l4)
    total = (lacc[3] + yr[0]) + (yr[1] + yr[2])
    lgo[...] = total[:, :LAT]
    rkgo[...] = total[:, LAT : LAT + ROPE]
    outs.append(on_device_copy(lgo, lg_hbm))
    outs.append(on_device_copy(rkgo, rkg_hbm))
    stage4(3)
    outs.append(on_device_copy(kugo, kug_hbm))
    outs.append(on_device_copy(vugo, vug_hbm))
    assert len(started) <= N_SEMS and n_local[0] <= 20
    for cp in started:
        cp.wait_send()
    for cp in outs:
        cp.wait()


def hand_over(*refs):
    sem = refs[12]
    copies = [pltpu.make_async_copy(a, b, sem.at[i]) for i, (a, b) in enumerate(zip(refs[:6], refs[6:12]))]
    for cp in copies:
        cp.start()
    for cp in copies:
        cp.wait()


def on_device(query_nope, query_rope, latent, rope_key, cotangent, bounds, key_up, value_up):
    shapes = [
        (SEQ, 512), (SEQ, 256), (8, LAT), (8, ROPE), (16, 512), (16, 512),
    ]
    out_shape = [jax.ShapeDtypeStruct(s, F32) for s in shapes]
    hbm = pl.BlockSpec(memory_space=pltpu.HBM)
    free = pl.BlockSpec(memory_space=pl.ANY)
    vm = lambda *s: pltpu.VMEM(s, F32)
    results = pl.pallas_call(
        kernel,
        out_shape=out_shape,
        in_specs=[hbm] * 5 + [pl.BlockSpec(memory_space=pltpu.SMEM)] + [hbm] * 2,
        out_specs=[free] * 6,
        scratch_shapes=[
            vm(SEQ, 512), vm(SEQ, 256), vm(SEQ, 512), vm(8, ROPE),
            vm(4, 8, 2, 2, 16, 256), vm(NYH, NZ, 8, LANES), vm(LAT, SEQ), vm(SEQ, 512), vm(SEQ, 256),
            vm(4, 16, 2, 16, 256), vm(4, 16, 16, 256), vm(4, 8, 2, 16, 256), vm(4, 8, 16, 256),
            vm(4, 8, 16, 256), vm(4, 7, 16, 256),
            vm(NYH, NZ, 8, LANES), vm(2, NYH, 8, LANES), vm(NYH, 8, LANES),
            vm(2, NYH, 8, LANES), vm(2, NYH, 8, LANES), vm(NYH, 8, LANES), vm(3, 8, LANES),
            vm(8, LAT), vm(8, ROPE), vm(16, 512), vm(16, 512),
            pltpu.SemaphoreType.DMA((N_SEMS,)),
            pltpu.SemaphoreType.DMA((N_SEMS,)),
            pltpu.SemaphoreType.DMA((20,)),
        ],
        compiler_params=pltpu.CompilerParams(
            collective_id=0, has_side_effects=True, vmem_limit_bytes=40 * 2**20
        ),
        name="fused",
    )(*[
        pltpu.with_memory_space_constraint(a, pltpu.HBM)
        for a in (query_nope, query_rope, latent, rope_key, cotangent, bounds, key_up, value_up)
    ])
    return pl.pallas_call(
        hand_over,
        out_shape=out_shape,
        in_specs=[free] * 6,
        out_specs=[hbm] * 6,
        scratch_shapes=[pltpu.SemaphoreType.DMA((6,))],
        compiler_params=pltpu.CompilerParams(vmem_limit_bytes=2 * 2**20),
        name="hand_over",
    )(*results)


def solution(mesh):
    return jax.shard_map(
        on_device,
        mesh=mesh,
        in_specs=(
            P("fsdp", "head"),
            P("fsdp", "head"),
            P(("fsdp", "head"), None),
            P(("fsdp", "head"), None),
            P("fsdp", "head"),
            P("fsdp", None),
            P("fsdp", "head"),
            P("fsdp", "head"),
        ),
        out_specs=(
            P("fsdp", "head"),
            P("fsdp", "head"),
            P(("fsdp", "head"), None),
            P(("fsdp", "head"), None),
            P("fsdp", "head"),
            P("fsdp", "head"),
        ),
        check_vma=False,
    )
```

```python
import jax
import jax.numpy as jnp
from jax import lax
from jax.experimental import pallas as pl
from jax.experimental.pallas import tpu as pltpu
from jax.sharding import PartitionSpec as P

NOPE = 128
ROPE = 64
VHEAD = 128
SEQ = 256
LAT = 512
LANES = 640
HEADS_HERE = 4
MESH = pl.DeviceIdType.MESH
F32 = jnp.float32
HIGH = lax.Precision.HIGH
FACTOR = (NOPE + ROPE) ** (-0.5)

NX, NYL, NC, NYH, NZ = 8, 2, 2, 4, 8


def dot_nn(a, b):
    return lax.dot_general(a, b, (((1,), (0,)), ((), ())), precision=HIGH, preferred_element_type=F32)


def dot_nt(a, b):
    return lax.dot_general(a, b, (((1,), (1,)), ((), ())), precision=HIGH, preferred_element_type=F32)


N_SEMS = 128


def kernel(
    qn_hbm, qr_hbm, lat_hbm, rk_hbm, cot_hbm, bounds_ref, ku_hbm, vu_hbm,
    qng_hbm, qrg_hbm, lg_hbm, rkg_hbm, kug_hbm, vug_hbm,
    qn, qr, cot, rk, wb, lb, latt, qng, qrg,
    ugb, sb, pb, yb, qb, xr,
    lgb, zr3, zr4, zr1, zr2, lacc, yr, lgo, rkgo, kugo, vugo,
    send, recv, local,
):
    f = lax.axis_index("fsdp")
    hd = lax.axis_index("head")
    x, y, c = f // 4, (f // 2) % 2, f % 2
    yh, z = hd // NZ, hd % NZ
    sgn = 1 - 2 * c

    def xi(dx):
        return (x + dx + 2 * NX) % NX

    def zi(dz):
        return (z + dz + 2 * NZ) % NZ

    def fx(dx):
        return ((xi(dx) * NYL + y) * NC + c, hd)

    def hz(dz):
        return (f, yh * NZ + zi(dz))

    def hy(r):
        return (f, (yh + r) % NYH * NZ + z)

    to_y = ((x * NYL + (1 - y)) * NC + c, hd)
    to_sib = ((x * NYL + y) * NC + (1 - c), hd)
    around = (2, -2, 3, -3, 4, 1, -1)

    n_local = [0]

    def on_device_copy(src, dst):
        cp = pltpu.make_async_copy(src, dst, local.at[n_local[0]])
        n_local[0] += 1
        cp.start()
        return cp

    started = []

    def push(src, dst, dev):
        k = len(started)
        cp = pltpu.make_async_remote_copy(
            src_ref=src, dst_ref=dst, send_sem=send.at[k], recv_sem=recv.at[k], device_id=dev, device_id_type=MESH
        )
        cp.start()
        started.append(cp)
        return cp

    def same(ref, dev):
        return push(ref, ref, dev)

    def landed(copies):
        for cp in copies:
            cp.wait_recv()

    own = [on_device_copy(lat_hbm, lb.at[0, z, :, pl.ds(0, LAT)]), on_device_copy(rk_hbm, rk)]
    for h in range(HEADS_HERE):
        own.append(on_device_copy(ku_hbm.at[:, pl.ds(h * NOPE, NOPE)], wb.at[h, x, y, c, :, pl.ds(0, NOPE)]))
        own.append(on_device_copy(vu_hbm.at[:, pl.ds(h * VHEAD, VHEAD)], wb.at[h, x, y, c, :, pl.ds(NOPE, VHEAD)]))
    later = [on_device_copy(qn_hbm, qn), on_device_copy(qr_hbm, qr), on_device_copy(cot_hbm, cot)]

    partners = [fx(d) for d in around] + [to_y, to_sib] + [hz(d) for d in around] + [hy(r) for r in (1, 2, 3)]
    barrier = pltpu.get_barrier_semaphore()
    for p in partners:
        pl.semaphore_signal(barrier, inc=1, device_id=p, device_id_type=MESH)
    for cp in own:
        cp.wait()
    lb[0, z, :, pl.ds(LAT, 128)] = jnp.concatenate([rk[...], jnp.zeros((8, 64), F32)], axis=1)
    pl.semaphore_wait(barrier, len(partners))

    ly = {r: push(lb.at[0, z], lb.at[NYH - r, z], hy(r)) for r in (1, 3, 2)}
    za = {d: same(lb.at[0, z], hz(d)) for d in around}
    xa, ya, sx, sy = {}, {}, {}, {}
    for h in range(HEADS_HERE):
        xa[h] = [same(wb.at[h, x, y, c], fx(d)) for d in around]
    zb = {d: [] for d in around}
    for r in (1, 3, 2):
        ly[r].wait_recv()
        for d in (2, -2, 1, -1):
            zb[d].append(same(lb.at[NYH - r, z], hz(d)))

    def row_over(h):
        landed(xa[h])
        ya[h] = same(wb.at[h, :, y, c], to_y)
        sx[h] = same(wb.at[h, :, y, c], to_sib)

    def other_row_over(h):
        ya[h].wait_recv()
        sy[h] = same(wb.at[h, :, 1 - y, c], to_sib)

    row_over(0)
    for d in (2, -2):
        landed(zb[d])
        zb[d + d // 2].append(same(lb.at[pl.ds(1, 3), zi(-d)], hz(d // 2)))
    zb[4].append(same(lb.at[pl.ds(1, 3), zi(-2 * sgn)], hz(2 * sgn)))
    row_over(1)
    other_row_over(0)
    row_over(2)
    for d in around:
        za[d].wait_recv()
    landed(zb[1] + zb[-1])
    landed(zb[3] + zb[-3] + zb[4])
    for cp in later:
        cp.wait()

    row_over(3)
    other_row_over(1)
    lat = lb[:, :, :, pl.ds(0, LAT)].reshape(SEQ, LAT)
    rope = lb[:, :, :, pl.ds(LAT, 128)].reshape(SEQ, 128)[:, :ROPE]

    row = lax.broadcasted_iota(jnp.int32, (SEQ, SEQ), 0)
    query = lax.broadcasted_iota(jnp.int32, (SEQ, SEQ), 1)
    turned = row + yh * 64
    key = jnp.where(turned >= SEQ, turned - SEQ, turned)
    visible = (key < bounds_ref[0, 1]) & ((key <= query) | (key < bounds_ref[0, 0]))

    s1, s2, s3 = {}, {}, {}

    def stage1(h):
        ugb[h] = dot_nn(latt[...], both[h]).reshape(16, 2, 16, 256)
        s1[h] = push(ugb.at[h, :, 1 - c], sb.at[h], to_sib)

    def stage2(h):
        s1[h].wait_recv()
        pb[h] = ugb[h, :, pl.ds(c, 1)].reshape(8, 2, 16, 256) + sb[h].reshape(8, 2, 16, 256)
        s2[h] = push(pb.at[h, :, 1 - y], yb.at[h], to_y)

    def stage3(h):
        s2[h].wait_recv()
        qb[h] = pb[h, :, pl.ds(y, 1)].reshape(8, 16, 256) + yb[h]
        s3[h] = [push(qb.at[h, xi(d)], xr.at[h, k], fx(d)) for k, d in enumerate(around)]

    def stage4(h):
        landed(s3[h])
        total = (qb[h, x] + xr[h, 0]) + (xr[h, 1] + xr[h, 2])
        total = total + ((xr[h, 3] + xr[h, 4]) + (xr[h, 5] + xr[h, 6]))
        kugo[:, pl.ds(h * NOPE, NOPE)] = total[:, :NOPE]
        vugo[:, pl.ds(h * VHEAD, VHEAD)] = total[:, NOPE:]

    both = {}
    rope_grads = []
    shared = latent_term = None
    for h in range(HEADS_HERE):
        landed([sx[h], sy[h]])
        up = wb[h].reshape(LAT, 256)
        kv = dot_nn(lat, up)
        if h == 0:
            latt[...] = lat.T
        kk = jnp.concatenate([kv[:, :NOPE], rope], axis=1)
        vv = kv[:, NOPE:]
        q = jnp.concatenate([qn[:, pl.ds(h * NOPE, NOPE)], qr[:, h * ROPE : (h + 1) * ROPE]], axis=1)
        ct = cot[:, pl.ds(h * VHEAD, VHEAD)]
        scores = dot_nt(kk, q) * FACTOR
        if h > 0:
            term = dot_nt(both[h - 1], up_before)
            latent_term = term if latent_term is None else latent_term + term
            ugb[h - 1] = dot_nn(latt[...], both[h - 1]).reshape(16, 2, 16, 256)
        scores = jnp.where(visible, scores, -jnp.inf)
        top = jnp.max(scores, axis=0, keepdims=True)
        attend = jnp.exp(scores - top)
        attend = attend * (1.0 / jnp.sum(attend, axis=0, keepdims=True))
        grad_attend = dot_nt(vv, ct)
        row_dot = jnp.sum(attend * grad_attend, axis=0, keepdims=True)
        grad_scores = attend * (grad_attend - row_dot) * FACTOR
        vg = dot_nn(attend, ct)
        kg = dot_nn(grad_scores, q)
        qg = dot_nn(grad_scores.T, kk)
        qng[:, pl.ds(h * NOPE, NOPE)] = qg[:, :NOPE]
        rope_grads.append(qg[:, NOPE:])
        shared = kg[:, NOPE:] if shared is None else shared + kg[:, NOPE:]
        both[h] = jnp.concatenate([kg[:, :NOPE], vg], axis=1)
        if h % 2 == 1:
            qrg[:, pl.ds((h - 1) * ROPE, 128)] = jnp.concatenate(rope_grads[-2:], axis=1)
        up_before = up
        if h > 0:
            s1[h - 1] = push(ugb.at[h - 1, :, 1 - c], sb.at[h - 1], to_sib)
        if h < 2:
            other_row_over(h + 2)
        if h > 1:
            stage2(h - 2)
    latent_term = latent_term + dot_nt(both[3], up_before)

    lgb[pl.ds(0, 3), :, :, pl.ds(0, LAT)] = latent_term[64:].reshape(3, NZ, 8, LAT)
    lgb[3, :, :, pl.ds(0, LAT)] = latent_term[:64].reshape(NZ, 8, LAT)
    shared = jnp.concatenate([shared, jnp.zeros((SEQ, 64), F32)], axis=1)
    lgb[pl.ds(0, 3), :, :, pl.ds(LAT, 128)] = shared[64:].reshape(3, NZ, 8, 128)
    lgb[3, :, :, pl.ds(LAT, 128)] = shared[:64].reshape(NZ, 8, 128)
    l3, l1 = {}, {}
    for g in (0, 1):
        part = pl.ds(2 * g, 2)
        l3[g] = [
            push(lgb.at[part, zi(4)], zr4.at[part], hz(2 * sgn)),
            push(lgb.at[part, zi(3)], zr3.at[0, part], hz(1)),
            push(lgb.at[part, zi(-3)], zr3.at[1, part], hz(-1)),
        ]
        l1[g] = [
            push(lgb.at[part, zi(1)], zr1.at[0, part], hz(1)),
            push(lgb.at[part, zi(-1)], zr1.at[1, part], hz(-1)),
        ]

    def latent_step2(g):
        landed(l3[g])
        part = pl.ds(2 * g, 2)
        for k, d in enumerate((2, -2)):
            at = (part, pl.ds(zi(d), 1))
            lgb[at] = lgb[at] + zr3[k, part].reshape(2, 1, 8, LANES)
        at = (part, pl.ds(zi(2 * sgn), 1))
        lgb[at] = lgb[at] + zr4[part].reshape(2, 1, 8, LANES)
        l1[g] += [push(lgb.at[part, zi(d)], zr2.at[k, part], hz(d)) for k, d in enumerate((2, -2))]

    l4 = []

    def latent_step3(g):
        landed(l1[g])
        part = pl.ds(2 * g, 2)
        lacc[part] = (
            lgb[part, pl.ds(z, 1)].reshape(2, 8, LANES) + (zr1[0, part] + zr1[1, part]) + (zr2[0, part] + zr2[1, part])
        )
        for p in (2 * g + 1, 2 * g):
            if p < 3:
                l4.append(push(lacc.at[p], yr.at[p], hy(p + 1)))

    outs = []
    stage1(3)
    stage2(2)
    outs.append(on_device_copy(qng, qng_hbm))
    outs.append(on_device_copy(qrg, qrg_hbm))
    stage3(0)
    stage2(3)
    stage3(1)
    latent_step2(0)
    stage3(2)
    latent_step2(1)
    stage3(3)
    latent_step3(0)
    latent_step3(1)
    stage4(0)
    stage4(1)
    stage4(2)
    landed(l4)
    total = (lacc[3] + yr[0]) + (yr[1] + yr[2])
    lgo[...] = total[:, :LAT]
    rkgo[...] = total[:, LAT : LAT + ROPE]
    outs.append(on_device_copy(lgo, lg_hbm))
    outs.append(on_device_copy(rkgo, rkg_hbm))
    stage4(3)
    outs.append(on_device_copy(kugo, kug_hbm))
    outs.append(on_device_copy(vugo, vug_hbm))
    assert len(started) <= N_SEMS and n_local[0] <= 20
    for cp in started:
        cp.wait_send()
    for cp in outs:
        cp.wait()


def hand_over(*refs):
    sem = refs[12]
    copies = [pltpu.make_async_copy(a, b, sem.at[i]) for i, (a, b) in enumerate(zip(refs[:6], refs[6:12]))]
    for cp in copies:
        cp.start()
    for cp in copies:
        cp.wait()


def on_device(query_nope, query_rope, latent, rope_key, cotangent, bounds, key_up, value_up):
    shapes = [
        (SEQ, 512), (SEQ, 256), (8, LAT), (8, ROPE), (16, 512), (16, 512),
    ]
    out_shape = [jax.ShapeDtypeStruct(s, F32) for s in shapes]
    hbm = pl.BlockSpec(memory_space=pltpu.HBM)
    free = pl.BlockSpec(memory_space=pl.ANY)
    vm = lambda *s: pltpu.VMEM(s, F32)
    results = pl.pallas_call(
        kernel,
        out_shape=out_shape,
        in_specs=[hbm] * 5 + [pl.BlockSpec(memory_space=pltpu.SMEM)] + [hbm] * 2,
        out_specs=[free] * 6,
        scratch_shapes=[
            vm(SEQ, 512), vm(SEQ, 256), vm(SEQ, 512), vm(8, ROPE),
            vm(4, 8, 2, 2, 16, 256), vm(NYH, NZ, 8, LANES), vm(LAT, SEQ), vm(SEQ, 512), vm(SEQ, 256),
            vm(4, 16, 2, 16, 256), vm(4, 16, 16, 256), vm(4, 8, 2, 16, 256), vm(4, 8, 16, 256),
            vm(4, 8, 16, 256), vm(4, 7, 16, 256),
            vm(NYH, NZ, 8, LANES), vm(2, NYH, 8, LANES), vm(NYH, 8, LANES),
            vm(2, NYH, 8, LANES), vm(2, NYH, 8, LANES), vm(NYH, 8, LANES), vm(3, 8, LANES),
            vm(8, LAT), vm(8, ROPE), vm(16, 512), vm(16, 512),
            pltpu.SemaphoreType.DMA((N_SEMS,)),
            pltpu.SemaphoreType.DMA((N_SEMS,)),
            pltpu.SemaphoreType.DMA((20,)),
        ],
        compiler_params=pltpu.CompilerParams(
            collective_id=0, has_side_effects=True, vmem_limit_bytes=40 * 2**20
        ),
        name="fused",
    )(*[
        pltpu.with_memory_space_constraint(a, pltpu.HBM)
        for a in (query_nope, query_rope, latent, rope_key, cotangent, bounds, key_up, value_up)
    ])
    return pl.pallas_call(
        hand_over,
        out_shape=out_shape,
        in_specs=[free] * 6,
        out_specs=[hbm] * 6,
        scratch_shapes=[pltpu.SemaphoreType.DMA((6,))],
        compiler_params=pltpu.CompilerParams(vmem_limit_bytes=2 * 2**20),
        name="hand_over",
    )(*results)


def solution(mesh):
    return jax.shard_map(
        on_device,
        mesh=mesh,
        in_specs=(
            P("fsdp", "head"),
            P("fsdp", "head"),
            P(("fsdp", "head"), None),
            P(("fsdp", "head"), None),
            P("fsdp", "head"),
            P("fsdp", None),
            P("fsdp", "head"),
            P("fsdp", "head"),
        ),
        out_specs=(
            P("fsdp", "head"),
            P("fsdp", "head"),
            P(("fsdp", "head"), None),
            P(("fsdp", "head"), None),
            P("fsdp", "head"),
            P("fsdp", "head"),
        ),
        check_vma=False,
    )
```
